256 devices in a mesh: cb: 4 (over x), tp: 64 (over z, y, core).
Axes of the slice: x: 4, y: 4, z: 8, core: 2. Of those that a mesh axis runs over, the one named last changes fastest.
Arguments:
- hidden_in: bfloat16 [1024, 4096], P('cb', 'tp'), may hold values from -6 to 6
- norm_gain: bfloat16 [4096], P('tp'), may hold values from 0.25 to 1.75
- w_qkv: bfloat16 [3, 4096, 4096], P(None, None, 'tp'), may hold values from -0.0625 to 0.0625
- w_out: bfloat16 [4096, 4096], P('tp'), may hold values from -0.09375 to 0.09375
- cache_keys: bfloat16 [1024, 64, 4096], P(('cb', 'tp')), may hold values from -6 to 6
- cache_values: bfloat16 [1024, 64, 4096], P(('cb', 'tp')), may hold values from -6 to 6
- lengths: int32 [1024], P(('cb', 'tp')), may hold values from 2 to 64, as said below
- tokens: int32 [1024, 8], P(None, 'cb'), may hold values from 0 to 2047
- w_in: bfloat16 [8, 4096, 1024], P('cb', 'tp'), may hold values from -0.09375 to 0.09375
- embed: bfloat16 [8, 2048, 1024], P('cb', None, 'tp'), may hold values from -6 to 6
- depth_gain: bfloat16 [8, 1024], P('cb'), may hold values from 0.25 to 1.75
- w_gate_up: bfloat16 [8, 2, 1024, 2816], P('cb', None, None, 'tp'), may hold values from -0.1875 to 0.1875
- w_down: bfloat16 [8, 2816, 1024], P('cb', 'tp'), may hold values from -0.109375 to 0.109375
Outputs:
- temporal_out: bfloat16 [1024, 4096], P('cb', 'tp')
- depth_out: bfloat16 [8, 1024, 1024], P('cb', None, 'tp')
The draws below stay inside these ranges and needn't reach their ends.
Inputs may be any that keep to these rules, and one draw needn't show every extreme that they name: `lengths`: number of live cache slots of each stream-beam; some row has all 64.
All inputs are finite; a program needn't handle non-finite values.
Results may differ from the reference program's by a relative error of at most 0.009.
Values may be sent and summed in bfloat16 or wider, within the bound.
No kernel may reach another device: no remote copies, remote signals or barrier semaphores. Data moves between devices by JAX's collectives and lax.ppermute only.
A program may use at most 64 MiB of HBM per device.

```python
import math
import jax
import jax.numpy as jnp
from jax import lax

D = 4096
HEADS = 32
HEAD_DIM = 128
DD = 1024
FD = 2816
CARD = 2048
NCB = 8
CACHE = 64
ROWS = 1024


def draw_lengths(key, part):
    key = jax.random.fold_in(key, 7)
    drawn = jax.random.randint(key, (ROWS,), 2, CACHE + 1, dtype=jnp.int32)
    return drawn.at[0].set(CACHE)


def draw_hidden_in(key, part):
    key = jax.random.fold_in(key, 11)
    key_drawn = jax.random.fold_in(key, 0)
    drawn = jnp.clip(jax.random.normal(key_drawn, (ROWS, D), jnp.float32), -6.0, 6.0)
    return drawn.astype(jnp.bfloat16)


def draw_w_qkv(key, part):
    key = jax.random.fold_in(key, 12)
    drawn = jnp.clip(jax.random.normal(key, (3, D, D), jnp.float32), -3.98, 3.98) / math.sqrt(D)
    return drawn.astype(jnp.bfloat16)


def draw_cache_keys(key, part):
    key = jax.random.fold_in(key, 13)
    drawn = jnp.clip(jax.random.normal(key, (ROWS, CACHE, D), jnp.float32), -6.0, 6.0)
    return drawn.astype(jnp.bfloat16)


def plant(values, rng, low, high):
    shape = values.shape
    place = [jax.random.randint(jax.random.fold_in(rng, axis), (), 0, shape[axis]) for axis in range(len(shape))]
    values = values.at[tuple(place)].set(low)
    longest = shape.index(max(shape))
    place[longest] = (place[longest] + 1) % shape[longest]
    return values.at[tuple(place)].set(high)


def level_of(stream_key, dims, cuts, least, high):
    def one(axis_at, blocks):
        draws = jax.random.uniform(jax.random.fold_in(jax.random.fold_in(stream_key, 6), axis_at), (blocks,), jnp.float32, least / len(cuts), high / len(cuts))
        return jnp.repeat(jnp.exp(draws), dims[axis_at] // blocks).reshape((-1,) + (1,) * (len(dims) - axis_at - 1))

    level = one(*cuts[0])
    for cut in cuts[1:]:
        level = level * one(*cut)
    return level


def centred(key, dims, width, most, cuts=(), kind=jnp.bfloat16):
    entries = width * jax.random.normal(key, dims, jnp.float32)
    if cuts:
        entries = entries * level_of(key, dims, cuts, -0.22, 0.18)
    return jnp.clip(entries, -most, most).astype(kind)


def setup_inputs(seed: int = 0) -> dict:
    splits = jax.random.split(jax.random.key(seed), 14)
    hidden_in = draw_hidden_in(jax.random.fold_in(splits[13], 71), 0)
    norm_gain = jnp.clip(1.0 + 0.15 * jax.random.normal(splits[1], (D,), jnp.float32), 0.25, 1.75).astype(jnp.bfloat16)
    w_qkv = draw_w_qkv(jax.random.fold_in(splits[13], 71), 0)
    w_out = centred(splits[3], (D, D), D ** -0.5, 0.09375, ((0, 64),))
    cache_keys = draw_cache_keys(jax.random.fold_in(splits[13], 71), 0)
    cache_values = centred(splits[5], (ROWS, CACHE, D), 1.0, 6.0, ((0, 256),))
    lengths = draw_lengths(jax.random.fold_in(splits[13], 71), 0)
    tokens = plant(jax.random.randint(splits[7], (ROWS, NCB), 0, CARD), jax.random.fold_in(splits[7], 1), 0, CARD - 1).astype(jnp.int32)
    w_in = centred(splits[8], (NCB, D, DD), D ** -0.5, 0.09375, ((0, 4), (1, 64)))
    embed = centred(splits[9], (NCB, CARD, DD), 1.0, 6.0, ((0, 4), (2, 64)))
    depth_gain = jnp.clip(1.0 + 0.15 * jax.random.normal(splits[10], (NCB, DD), jnp.float32), 0.25, 1.75).astype(jnp.bfloat16)
    w_gate_up = centred(splits[11], (NCB, 2, DD, FD), DD ** -0.5, 0.1875, ((0, 4), (3, 64)))
    w_down = centred(splits[12], (NCB, FD, DD), FD ** -0.5, 0.109375, ((0, 4), (1, 64)))
    return dict(hidden_in=hidden_in, norm_gain=norm_gain, w_qkv=w_qkv, w_out=w_out, cache_keys=cache_keys, cache_values=cache_values, lengths=lengths, tokens=tokens, w_in=w_in, embed=embed, depth_gain=depth_gain, w_gate_up=w_gate_up, w_down=w_down)


eps = 1e-05

def attend_block(args):
    query, key_new, value_new, keys, values, lens = args
    rows = query.shape[0]
    scale = 1.0 / math.sqrt(HEAD_DIM)
    query_h = query.astype(jnp.float32).reshape(rows, HEADS, HEAD_DIM)
    keys_h = keys.astype(jnp.float32).reshape(rows, CACHE, HEADS, HEAD_DIM)
    values_h = values.astype(jnp.float32).reshape(rows, CACHE, HEADS, HEAD_DIM)
    scores = jnp.einsum('rhe,rphe->rhp', query_h, keys_h) * scale
    live = jnp.arange(CACHE)[None, None, :] < lens[:, None, None]
    scores = jnp.where(live, scores, -1e+30)
    fresh = lax.optimization_barrier(jnp.sum(query_h * key_new.astype(jnp.float32).reshape(rows, HEADS, HEAD_DIM), axis=-1)) * scale
    top = jnp.maximum(lax.optimization_barrier(jnp.max(scores, axis=-1)), fresh)
    weights = jnp.exp(scores - top[..., None])
    weight_new = jnp.exp(fresh - top)
    total = lax.optimization_barrier(jnp.sum(weights, axis=-1)) + weight_new
    probs = (weights / total[..., None]).astype(jnp.bfloat16)
    prob_new = (weight_new / total).astype(jnp.bfloat16)
    mixed = jnp.einsum('rhp,rphe->rhe', probs.astype(jnp.float32), values_h)
    mixed = mixed + prob_new.astype(jnp.float32)[..., None] * value_new.astype(jnp.float32).reshape(rows, HEADS, HEAD_DIM)
    return mixed.reshape(rows, D).astype(jnp.bfloat16)

def reference(hidden_in, norm_gain, w_qkv, w_out, cache_keys, cache_values, lengths, tokens, w_in, embed, depth_gain, w_gate_up, w_down):
    hid32 = hidden_in.astype(jnp.float32)
    mean_sq = lax.optimization_barrier(jnp.mean(hid32 * hid32, axis=1))
    normed = (hid32 * lax.rsqrt(mean_sq + eps)[:, None] * norm_gain.astype(jnp.float32)).astype(jnp.bfloat16)
    qkv = jnp.einsum('rd,idf->rif', normed.astype(jnp.float32), w_qkv.astype(jnp.float32)).astype(jnp.bfloat16)
    block = math.gcd(ROWS, 64)
    count = ROWS // block
    attended = lax.map(attend_block, (qkv[:, 0].reshape(count, block, D), qkv[:, 1].reshape(count, block, D), qkv[:, 2].reshape(count, block, D), cache_keys.reshape(count, block, CACHE, D), cache_values.reshape(count, block, CACHE, D), lengths.reshape(count, block)))
    attended = attended.reshape(ROWS, D)
    temporal_out = (hid32 + jnp.dot(attended, w_out, preferred_element_type=jnp.float32)).astype(jnp.bfloat16)
    results = []
    for step in range(NCB):
        before = (step - 1) % NCB
        token_rows = embed[before][tokens[:, before]].astype(jnp.float32)
        x_step = jnp.dot(temporal_out, w_in[step], preferred_element_type=jnp.float32) + token_rows
        mean_d = lax.optimization_barrier(jnp.mean(x_step * x_step, axis=1))
        xn_step = (x_step * lax.rsqrt(mean_d + eps)[:, None] * depth_gain[step].astype(jnp.float32)).astype(jnp.bfloat16)
        gate = jnp.dot(xn_step, w_gate_up[step, 0], preferred_element_type=jnp.float32)
        upper = jnp.dot(xn_step, w_gate_up[step, 1], preferred_element_type=jnp.float32)
        act = (jax.nn.silu(gate) * upper).astype(jnp.bfloat16)
        results.append((x_step + jnp.dot(act, w_down[step], preferred_element_type=jnp.float32)).astype(jnp.bfloat16))
    return (temporal_out, jnp.stack(results))
```

```python
import math

import jax
import jax.numpy as jnp
from jax import lax
from jax.sharding import Mesh, PartitionSpec as P

D = 4096
HEADS = 32
HEAD_DIM = 128
DD = 1024
CARD = 2048
CACHE = 64
X, Z, Y, C = 4, 8, 4, 2
HID = 44
HID_PAD = 96

eps = 1e-05
BF = jnp.bfloat16
F32 = jnp.float32
TP = ("z", "y", "core")


def exchange(value, axis):
    return lax.all_to_all(value, axis, split_axis=0, concat_axis=0, tiled=True)


def spread(value, axis):
    count = lax.axis_size(axis)
    copies = jnp.broadcast_to(value[None], (count,) + value.shape)
    return exchange(copies, axis)


def swap(value):
    return lax.ppermute(value, "core", [(0, 1), (1, 0)])


def pick(value, index):
    return lax.dynamic_index_in_dim(value, index, 0, keepdims=False)


def per_device(
    hidden_in,
    norm_gain,
    w_qkv,
    w_out,
    cache_keys,
    cache_values,
    lengths,
    tokens,
    w_in,
    embed,
    depth_gain,
    w_gate_up,
    w_down,
):
    xi, zi, yi, ci = (lax.axis_index(a) for a in ("cb", "z", "y", "core"))
    other = 1 - ci

    with jax.named_scope("pack_weights"):
        emb_t = embed.transpose(0, 2, 1)
        emb_r = jnp.concatenate([emb_t[:, :, :DD], emb_t[:, :, DD:]], axis=1)
        keep_a = jnp.concatenate([pick(w_in, ci), pick(emb_r, other)], axis=0)
        send_a = jnp.concatenate([pick(w_in, other), pick(emb_r, ci)], axis=0)
        recv_a = swap(send_a)
        wo = lax.dynamic_slice_in_dim(w_out, xi * DD, DD, 1)
        wo = wo.reshape(64, 2, 8, 64).transpose(0, 2, 1, 3).reshape(64, DD)
        first = lax.all_gather(jnp.concatenate([wo, keep_a, recv_a], axis=0), "z")
        gu_t = w_gate_up.transpose(0, 3, 1, 2)
        own_gu, own_dn = pick(gu_t, ci), pick(w_down, ci)
        send_b = jnp.concatenate(
            [pick(gu_t, other)[:, 0], pick(gu_t, other)[:, 1], pick(w_down, other)], axis=0
        )
        recv_b = swap(send_b)
        fill = jnp.zeros((HID_PAD - 2 * HID, DD), BF)
        second = lax.all_gather(
            jnp.concatenate(
                [
                    own_gu[:, 0],
                    recv_b[:HID],
                    fill,
                    own_gu[:, 1],
                    recv_b[HID : 2 * HID],
                    fill,
                    own_dn,
                    recv_b[2 * HID :],
                    fill,
                ],
                axis=0,
            ),
            "z",
        )

    with jax.named_scope("gather_hidden"):
        gain_row = jnp.pad(norm_gain[None, :], ((0, 7), (0, 192)))
        shard = jnp.concatenate([hidden_in.T, gain_row], axis=0)
        mine = spread(spread(shard, "z"), "y")
        theirs = swap(mine)
        core0 = jnp.where(ci == 0, mine, theirs)
        core1 = jnp.where(ci == 0, theirs, mine)
        both = jnp.stack([core0, core1], axis=0).transpose(2, 1, 0, 3, 4)
        hid = both[:, :, :, :64, :].astype(F32)
        gain = both[:, :, :, 64, :64].astype(F32)
        sum_sq = jnp.sum(hid * hid, axis=(0, 1, 2, 3))
        normed = (hid * lax.rsqrt(sum_sq / D + eps) * gain[..., None]).astype(BF)
        normed = normed.reshape(D, 256)

    with jax.named_scope("qkv"):
        qkv = jnp.einsum("dr,idf->rif", normed, w_qkv, preferred_element_type=F32).astype(BF)
        sent = jnp.concatenate([qkv.reshape(256, 192), hidden_in], axis=1)
        got = exchange(sent.reshape(64, 4, 256), TP)
        got = got.reshape(HEADS, 2, 4, 4, 64).transpose(2, 3, 0, 1, 4)
        got = got.reshape(4, 4, HEADS, HEAD_DIM)

    with jax.named_scope("attend"):
        query_h, key_new, value_new = got[:, 0], got[:, 1], got[:, 2]
        hid_rows = got[:, 3]
        scale = 1.0 / math.sqrt(HEAD_DIM)
        keys_h = cache_keys.reshape(4, CACHE, HEADS, HEAD_DIM)
        values_h = cache_values.reshape(4, CACHE, HEADS, HEAD_DIM)
        scores = jnp.einsum("rhe,rphe->rhp", query_h, keys_h, preferred_element_type=F32) * scale
        live = lax.broadcasted_iota(jnp.int32, (1, 1, CACHE), 2) < lengths[:, None, None]
        scores = jnp.where(live, scores, -1e30)
        fresh = jnp.sum(query_h.astype(F32) * key_new.astype(F32), axis=-1) * scale
        top = jnp.maximum(jnp.max(scores, axis=-1), fresh)
        weights = jnp.exp(scores - top[..., None])
        weight_new = jnp.exp(fresh - top)
        total = jnp.sum(weights, axis=-1) + weight_new
        probs = (weights / total[..., None]).astype(BF)
        prob_new = (weight_new / total).astype(BF)
        mixed = jnp.einsum("rhp,rphe->rhe", probs, values_h, preferred_element_type=F32)
        mixed = mixed + prob_new.astype(F32)[..., None] * value_new.astype(F32)
        attended = mixed.astype(BF)

    with jax.named_scope("project"):
        att = attended.reshape(4, Z, Y, C, 64).transpose(2, 3, 0, 1, 4).reshape(1, 8, 4, 512)
        att = jnp.broadcast_to(att, (X, 8, 4, 512))
        res = hid_rows.reshape(4, X, 2, Y, C, 64).transpose(1, 3, 4, 0, 2, 5)
        res = res.reshape(X, 8, 4, 128)
        moved = exchange(
            jnp.concatenate([att, res], axis=-1).reshape(32, 4, 640), ("cb", "y", "core")
        ).reshape(128, 640)
        wo_rows = first[:, :64].reshape(512, DD)
        part = jnp.dot(moved[:, :512], wo_rows, preferred_element_type=F32).astype(BF)
        part = exchange(part.reshape(128, 8, 128).transpose(1, 0, 2), ("y", "core"))
        temporal = jnp.sum(part.astype(F32), axis=0) + moved[:, 512:].astype(F32)
        temporal = temporal.astype(BF)
        frame = spread(temporal, "cb")
        frame_all = jnp.concatenate([frame, swap(frame)], axis=0)

    with jax.named_scope("embed"):
        token = lax.dynamic_index_in_dim(tokens, other, 1, keepdims=False)
        token = lax.dynamic_index_in_dim(token.reshape(X, Z, 32), zi, 1, keepdims=False)
        codes = lax.broadcasted_iota(jnp.int32, (2, DD, 1), 1) + DD * lax.broadcasted_iota(
            jnp.int32, (2, DD, 1), 0
        )
        one_hot = (codes == token.reshape(1, 1, 128)).astype(BF)
        tables = jnp.stack([first[:, 128:160], first[:, 224:256]], axis=0)
        tables = tables.reshape(2, Z, 2, 16, DD)
        emb = jnp.einsum("czhft,htr->czfr", tables, one_hot, preferred_element_type=F32)
        emb = emb.astype(BF)
        moved_emb = lax.ppermute(
            emb, ("cb", "core"), [(2 * x, 2 * ((x + 1) % X)) for x in range(X)]
        )
        emb = jnp.where(ci == 0, moved_emb, emb)
        emb0 = jnp.where(ci == 0, emb[0], emb[1])
        emb1 = jnp.where(ci == 0, emb[1], emb[0])
        emb = jnp.stack([emb0, emb1], axis=1)[:, None]
        here = lax.broadcasted_iota(jnp.int32, (1, Y, 1, 1, 1), 1) == yi
        emb = jnp.where(here, emb, jnp.zeros((), BF)).reshape(DD, 128)

    with jax.named_scope("depth_in"):
        win = jnp.concatenate([first[:, 64:128], first[:, 160:224]], axis=0)
        win = win.reshape(8, 128, DD)
        x_part = jnp.einsum("brk,bkn->nr", frame_all, win, preferred_element_type=F32)
        x_part = (x_part + emb.astype(F32)).astype(BF)
        x = jnp.sum(spread(x_part, "y").astype(F32), axis=0)

    with jax.named_scope("depth_ff"):
        mean = jnp.sum(x * x, axis=0) / DD
        gain_d = pick(depth_gain, ci).astype(F32)
        xn = (x * lax.rsqrt(mean + eps) * gain_d[:, None]).astype(BF)
        gate = jnp.einsum(
            "zhd,dr->zhr", second[:, :HID_PAD], xn, preferred_element_type=F32
        )
        upper = jnp.einsum(
            "zhd,dr->zhr", second[:, HID_PAD : 2 * HID_PAD], xn, preferred_element_type=F32
        )
        act = (jax.nn.silu(gate) * upper).astype(BF)
        down = jnp.einsum(
            "zhn,zhr->nr", second[:, 2 * HID_PAD :], act, preferred_element_type=F32
        )
        out = (down + x * (1.0 / Y)).astype(BF)
        out = exchange(out.reshape(Z, Y, 32, 128).transpose(1, 0, 2, 3), "y")
        out = jnp.sum(out.astype(F32), axis=0).astype(BF).reshape(Z, C, 16, 128)

    with jax.named_scope("place_outputs"):
        rows = lax.dynamic_slice_in_dim(frame, xi * 32, 32, 1)
        rows = rows.reshape(X, 2, 16, 2, 64).transpose(0, 3, 2, 1, 4).reshape(Z, 1, 16, 128)
        same = lax.broadcasted_iota(jnp.int32, (1, C, 1, 1), 1) == ci
        rows = jnp.where(same, rows, jnp.zeros((), BF))
        last = exchange(jnp.concatenate([out, rows], axis=2).reshape(16, 32, 128), ("z", "core"))
        last = last.reshape(Z, C, 32, 128)
        depth_out = last[:, :, :16].reshape(Z, C, 16, X, 32).transpose(1, 3, 0, 4, 2)
        depth_out = depth_out.reshape(C, 1024, 16)
        temporal_out = lax.dynamic_index_in_dim(last[:, :, 16:], ci, 1, keepdims=False)
        temporal_out = temporal_out.reshape(Z, 16, 2, 64).transpose(0, 2, 1, 3).reshape(256, 64)
    return (temporal_out, depth_out)


def solution(mesh):
    fine = Mesh(mesh.devices.reshape(X, Z, Y, C), ("cb", "z", "y", "core"))
    every = ("cb",) + TP
    in_specs = (
        P("cb", TP),
        P(TP),
        P(None, None, TP),
        P(TP, None),
        P(every, None, None),
        P(every, None, None),
        P(every),
        P(None, "cb"),
        P("cb", TP, None),
        P("cb", None, TP),
        P("cb", None),
        P("cb", None, None, TP),
        P("cb", TP, None),
    )
    out_specs = (P("cb", TP), P("cb", None, TP))
    return jax.shard_map(
        per_device, mesh=fine, in_specs=in_specs, out_specs=out_specs, check_vma=False
    )
```

```python
import math

import jax
import jax.numpy as jnp
from jax import lax
from jax.experimental import pallas as pl
from jax.experimental.pallas import tpu as pltpu
from jax.sharding import Mesh, PartitionSpec as P

D = 4096
HEADS = 32
HEAD_DIM = 128
DD = 1024
CARD = 2048
CACHE = 64
X, Z, Y, C = 4, 8, 4, 2
HID = 44
HID_PAD = 48

eps = 1e-05
BF = jnp.bfloat16
F32 = jnp.float32
TP = ("z", "y", "core")


def exchange(value, axis):
    return lax.all_to_all(value, axis, split_axis=0, concat_axis=0, tiled=True)


def spread(value, axis):
    count = lax.axis_size(axis)
    copies = jnp.broadcast_to(value[None], (count,) + value.shape)
    return exchange(copies, axis)


def from_each(value, axis):
    count = lax.axis_size(axis)
    return [value] + [
        lax.ppermute(value, axis, [(i, (i + step) % count) for i in range(count)])
        for step in range(1, count)
    ]


def ring_halves(low, high, axis):
    up = [(i, (i + 1) % 4) for i in range(4)]
    down = [(i, (i + 3) % 4) for i in range(4)]
    low_behind = lax.ppermute(low, axis, up)
    high_ahead = lax.ppermute(high, axis, down)
    high_behind = lax.ppermute(high, axis, up)
    low_ahead = lax.ppermute(low, axis, down)
    low_across = lax.ppermute(low_behind, axis, up)
    high_across = lax.ppermute(high_ahead, axis, down)
    return (low_behind, high_behind), (low_ahead, high_ahead), (low_across, high_across)


def swap(value):
    return lax.ppermute(value, "core", [(0, 1), (1, 0)])


def pick(value, index):
    return lax.dynamic_index_in_dim(value, index, 0, keepdims=False)


def dot_nt(a, b):
    return lax.dot_general(a, b, (((1,), (1,)), ((), ())), preferred_element_type=F32)


def in_vmem(kernel, out_shape, flops, args):
    return pl.pallas_call(
        kernel,
        in_specs=[pl.BlockSpec(memory_space=pltpu.VMEM)] * len(args),
        out_specs=pl.BlockSpec(memory_space=pltpu.VMEM),
        out_shape=jax.ShapeDtypeStruct(out_shape, BF),
        compiler_params=pltpu.CompilerParams(vmem_limit_bytes=24 * 1024 * 1024),
        cost_estimate=pl.CostEstimate(
            flops=flops, bytes_accessed=sum(a.size * 2 for a in args), transcendentals=0
        ),
    )(*args)


def prepare_kernel(hid_ref, emb_ref, token_ref, hid_out, emb_out):
    row = lax.broadcasted_iota(jnp.int32, (256, 256), 0)
    col = lax.broadcasted_iota(jnp.int32, (256, 256), 1)
    within = col % 128
    chosen = (row == (within // 4) * 8 + within % 4 + 4 * (col // 128)).astype(BF)
    split = jnp.dot(hid_ref[...], chosen, preferred_element_type=F32).astype(BF)
    hid_out[0] = split[:, :128]
    hid_out[1] = split[:, 128:]
    low_codes = lax.broadcasted_iota(jnp.int32, (128, 1024), 0)
    for core in range(C):
        index = 1 - core
        token = token_ref[index : index + 1]
        low = (low_codes == token % 128).astype(BF)
        high = token // 128
        table = jnp.concatenate(
            [emb_ref[index, :, h * 128 : (h + 1) * 128] for h in range(16)], axis=0
        )
        found = jnp.dot(table, low, preferred_element_type=F32)
        total = jnp.zeros((16, 1024), F32)
        for h in range(16):
            total += jnp.where(high == h, found[h * 16 : (h + 1) * 16], 0.0)
        for z in range(Z):
            emb_out[z, core] = jnp.concatenate(
                [total[:, x * 256 + z * 32 : x * 256 + z * 32 + 32] for x in range(X)], axis=1
            ).astype(BF)


def prepare(hid_t, emb_t, token):
    return pl.pallas_call(
        prepare_kernel,
        in_specs=[pl.BlockSpec(memory_space=pltpu.VMEM)] * 3,
        out_specs=[pl.BlockSpec(memory_space=pltpu.VMEM)] * 2,
        out_shape=[
            jax.ShapeDtypeStruct((C, 64, 128), BF),
            jax.ShapeDtypeStruct((Z, C, 16, 128), BF),
        ],
        compiler_params=pltpu.CompilerParams(vmem_limit_bytes=24 * 1024 * 1024),
    )(hid_t, emb_t, token)


def project_kernel(moved_ref, w_ref, out_ref):
    acc = jnp.zeros((128, DD), F32)
    for i in range(4):
        acc += jnp.dot(
            moved_ref[:, i * 128 : (i + 1) * 128],
            w_ref[2 * i : 2 * i + 2, 128:].reshape(128, DD),
            preferred_element_type=F32,
        )
    for block in range(8):
        low = acc[:, block * 64 : (block + 1) * 64]
        high = acc[:, 512 + block * 64 : 512 + (block + 1) * 64]
        out_ref[block] = jnp.concatenate([low, high], axis=1).astype(BF)


def depth_in_kernel(own_ref, oth_ref, w_ref, emb_ref, out_ref):
    acc = emb_ref[...].astype(F32)
    for i in range(X):
        w = w_ref[2 * i : 2 * i + 2, :128]
        acc += jnp.dot(own_ref[i], w[:, :64].reshape(128, DD), preferred_element_type=F32)
        acc += jnp.dot(oth_ref[i], w[:, 64:].reshape(128, DD), preferred_element_type=F32)
    out_ref[...] = acc.astype(BF)


def depth_ff_kernel(a_ref, b_ref, c_ref, d_ref, gain_ref, w_ref, out_ref):
    x = a_ref[...].astype(F32) + b_ref[...].astype(F32)
    x = x + c_ref[...].astype(F32) + d_ref[...].astype(F32)
    mean = jnp.sum(x * x, axis=1, keepdims=True) / DD
    xn = (x * lax.rsqrt(mean + eps) * gain_ref[...]).astype(BF)
    acc = x * (1.0 / Y)
    wide = 2 * HID_PAD
    for i in range(4):
        w = w_ref.at[2 * i : 2 * i + 2]
        gate = dot_nt(xn, w[:, :wide].reshape(2 * wide, DD))
        upper = dot_nt(xn, w[:, wide : 2 * wide].reshape(2 * wide, DD))
        act = (jax.nn.silu(gate) * upper).astype(BF)
        acc += jnp.dot(
            act, w[:, 2 * wide :].reshape(2 * wide, DD), preferred_element_type=F32
        )
    for block in range(Z):
        turned = acc[:, block * 128 : (block + 1) * 128].T
        out_ref[block] = turned.reshape(Y, 32, 128).astype(BF)


def per_device(
    hidden_in,
    norm_gain,
    w_qkv,
    w_out,
    cache_keys,
    cache_values,
    lengths,
    tokens,
    w_in,
    embed,
    depth_gain,
    w_gate_up,
    w_down,
):
    xi, zi, yi, ci = (lax.axis_index(a) for a in ("cb", "z", "y", "core"))
    other = 1 - ci

    with jax.named_scope("gather_hidden"):
        hid_split, emb_sent = prepare(hidden_in.T, embed.transpose(0, 2, 1), tokens.T)
        gain_row = jnp.pad(norm_gain[None, :], ((0, 7), (0, 64)))
        copies = jnp.concatenate(
            [
                jnp.broadcast_to(hid_split[None], (Z, C, 64, 128)),
                jnp.broadcast_to(gain_row, (Z, C, 8, 128)),
                emb_sent,
            ],
            axis=2,
        )
        column = exchange(copies.reshape(16, 88, 128), ("z", "core")).reshape(Z, C, 88, 128)
        emb_here = column[:, :, 72:]
        started = swap(hid_split[0, :16])
        w_in, w_out, w_gate_up, w_down, w_qkv, started = lax.optimization_barrier(
            (w_in, w_out, w_gate_up, w_down, w_qkv, started)
        )

    with jax.named_scope("pack_weights"):
        recv_a = swap(pick(w_in, other))
        wo = lax.dynamic_slice_in_dim(w_out, xi * DD, DD, 1)
        first_in = jnp.concatenate([pick(w_in, ci), recv_a, wo], axis=0)
        gu_t = w_gate_up.transpose(0, 3, 1, 2)
        gap = ((0, HID_PAD - HID), (0, 0))

        def stacked(step):
            gu = pick(gu_t, step)
            parts = (gu[:, 0], gu[:, 1], pick(w_down, step))
            return [jnp.pad(part, gap) for part in parts]

        recv_b = swap(jnp.concatenate(stacked(other), axis=0))
        second_in = []
        for index, part in enumerate(stacked(ci)):
            second_in += [part, recv_b[index * HID_PAD : (index + 1) * HID_PAD]]
        second_in = jnp.concatenate(second_in, axis=0)
        first = lax.all_gather(first_in, "z")
        second = lax.all_gather(second_in, "z")

    with jax.named_scope("norm"):
        w_own = w_qkv.transpose(0, 2, 1).reshape(192, D)
        w_oth = swap(w_own)
        halves = (column[:4, :, :72], column[4:, :, :72])
        pieces = [(halves, 0)] + list(zip(ring_halves(*halves, "y"), (3, 1, 2)))
        blocks = [
            (part, index * 4, lax.rem(yi + step, Y))
            for parts, step in pieces
            for index, part in enumerate(parts)
        ]
        sum_sq = sum(
            jnp.sum(jnp.square(part[:, :, :64].astype(F32)), axis=(0, 1, 2))
            for part, _, _ in blocks
        )
        inv = lax.rsqrt(sum_sq / D + eps)
        normed = jnp.zeros((Z, Y, C, 64, 128), BF)
        for part, at_z, at_y in blocks:
            gain = part[:, :, 64, :64].astype(F32)[..., None]
            block = (part[:, :, :64].astype(F32) * inv * gain).astype(BF)
            normed = lax.dynamic_update_slice(normed, block[:, None], (at_z, at_y, 0, 0, 0))
        normed = normed.reshape(D, 128)

    with jax.named_scope("qkv"):
        q_own = jnp.einsum("dr,nd->rn", normed, w_own, preferred_element_type=F32).astype(BF)
        q_oth = jnp.einsum("dr,nd->rn", normed, w_oth, preferred_element_type=F32).astype(BF)
        q_low = jnp.where(ci == 0, q_own, q_oth).reshape(128, 3, 64)
        q_high = jnp.where(ci == 0, q_oth, q_own).reshape(128, 3, 64)
        hid_cols = pick(column, zi)[:, :64]
        qkv = jnp.concatenate([q_low, q_high], axis=2).reshape(128, 384)
        sent = jnp.concatenate([qkv, hid_cols.reshape(128, 128).T], axis=1)
        got = exchange(sent.reshape(32, 4, 512), ("z", "y"))
        got = got.reshape(HEADS, 4, 4, HEAD_DIM).transpose(1, 2, 0, 3)

    with jax.named_scope("embed"):
        moved_emb = lax.ppermute(
            emb_here, ("cb", "core"), [(2 * x, 2 * ((x + 1) % X)) for x in range(X)]
        )
        emb = jnp.where(ci == 0, moved_emb, emb_here).reshape(256, 128)
        source = lax.broadcasted_iota(jnp.int32, (256, DD), 0)
        target = lax.broadcasted_iota(jnp.int32, (256, DD), 1)
        place = (target == (source // 32) * 128 + yi * 32 + source % 32).astype(BF)
        emb = jnp.dot(emb.T, place, preferred_element_type=F32).astype(BF)

    with jax.named_scope("attend"):
        got, first = lax.optimization_barrier((got, first))
        query_h, key_new, value_new = got[:, 0], got[:, 1], got[:, 2]
        hid_rows = got[:, 3]
        scale = 1.0 / math.sqrt(HEAD_DIM)
        keys_h = cache_keys.reshape(4, CACHE, HEADS, HEAD_DIM)
        values_h = cache_values.reshape(4, CACHE, HEADS, HEAD_DIM)
        scores = jnp.einsum("rhe,rphe->rhp", query_h, keys_h, preferred_element_type=F32) * scale
        live = lax.broadcasted_iota(jnp.int32, (1, 1, CACHE), 2) < lengths[:, None, None]
        scores = jnp.where(live, scores, -1e30)
        fresh = jnp.sum(query_h.astype(F32) * key_new.astype(F32), axis=-1) * scale
        top = jnp.maximum(jnp.max(scores, axis=-1), fresh)
        weights = jnp.exp(scores - top[..., None])
        weight_new = jnp.exp(fresh - top)
        total = jnp.sum(weights, axis=-1) + weight_new
        probs = (weights / total[..., None]).astype(BF)
        prob_new = (weight_new / total).astype(BF)
        mixed = jnp.einsum("rhp,rphe->rhe", probs, values_h, preferred_element_type=F32)
        mixed = mixed + prob_new.astype(F32)[..., None] * value_new.astype(F32)
        attended = mixed.astype(BF)

    with jax.named_scope("project"):
        att = attended.reshape(4, Z, Y, C, 64).transpose(2, 3, 0, 1, 4).reshape(1, 8, 4, 512)
        att = jnp.broadcast_to(att, (X, 8, 4, 512))
        res = hid_rows.reshape(4, X, 2, Y, C, 64).transpose(1, 3, 4, 0, 2, 5)
        res = res.reshape(X, 8, 4, 128)
        moved = exchange(
            jnp.concatenate([att, res], axis=-1).reshape(32, 4, 640), ("cb", "y", "core")
        ).reshape(128, 640)
        part = in_vmem(project_kernel, (8, 128, 128), 2 * 128 * 512 * DD, (moved[:, :512], first))
        part = exchange(part, ("y", "core"))
        temporal = jnp.sum(part.astype(F32), axis=0) + moved[:, 512:].astype(F32)
        temporal = temporal.astype(BF)
        around = from_each(temporal, "cb")
        frame = jnp.zeros((X, 128, 128), BF)
        for step, piece in enumerate(around):
            at = lax.rem(xi - step + X, X)
            frame = lax.dynamic_update_slice(frame, piece[None], (at, 0, 0))
        frame_oth = swap(frame)

    with jax.named_scope("depth"):
        x_part = in_vmem(
            depth_in_kernel, (128, DD), 2 * 128 * 1024 * DD, (frame, frame_oth, first, emb)
        )
        gain_d = lax.dynamic_slice_in_dim(depth_gain, ci, 1, 0).astype(F32)
        out = in_vmem(
            depth_ff_kernel,
            (Z, Y, 32, 128),
            6 * 128 * 768 * DD,
            (*from_each(x_part, "y"), gain_d, second),
        )
        out = exchange(out.reshape(64, 16, 128), TP).reshape(Z, Y, C, 16, 128)
        out = jnp.sum(out.astype(F32), axis=1).astype(BF)

    with jax.named_scope("place_outputs"):
        depth_out = out.reshape(Z, C, 16, X, 32).transpose(1, 3, 0, 4, 2)
        depth_out = depth_out.reshape(C, 1024, 16)
        rows = lax.dynamic_slice_in_dim(frame, xi * 32, 32, 1)
        rows = rows.reshape(X, 2, 16, 2, 64).transpose(0, 3, 2, 1, 4).reshape(Z, 16, 128)
        rows = exchange(rows, "z")
        temporal_out = rows.reshape(Z, 16, 2, 64).transpose(0, 2, 1, 3).reshape(256, 64)
    return (temporal_out, depth_out)


def solution(mesh):
    fine = Mesh(mesh.devices.reshape(X, Z, Y, C), ("cb", "z", "y", "core"))
    every = ("cb",) + TP
    in_specs = (
        P("cb", TP),
        P(TP),
        P(None, None, TP),
        P(TP, None),
        P(every, None, None),
        P(every, None, None),
        P(every),
        P(None, "cb"),
        P("cb", TP, None),
        P("cb", None, TP),
        P("cb", None),
        P("cb", None, None, TP),
        P("cb", TP, None),
    )
    out_specs = (P("cb", TP), P("cb", None, TP))
    return jax.shard_map(
        per_device, mesh=fine, in_specs=in_specs, out_specs=out_specs, check_vma=False
    )
```

```python
import math

import jax
import jax.numpy as jnp
from jax import lax
from jax.experimental import pallas as pl
from jax.experimental.pallas import tpu as pltpu
from jax.sharding import Mesh, PartitionSpec as P

D = 4096
HEADS = 32
HEAD_DIM = 128
DD = 1024
CARD = 2048
CACHE = 64
X, Z, Y, C = 4, 8, 4, 2
HID = 44
HID_PAD = 48

eps = 1e-05
BF = jnp.bfloat16
F32 = jnp.float32
TP = ("z", "y", "core")


def exchange(value, axis):
    return lax.all_to_all(value, axis, split_axis=0, concat_axis=0, tiled=True)


def spread(value, axis):
    count = lax.axis_size(axis)
    copies = jnp.broadcast_to(value[None], (count,) + value.shape)
    return exchange(copies, axis)


def from_each(value, axis):
    count = lax.axis_size(axis)
    return [value] + [
        lax.ppermute(value, axis, [(i, (i + step) % count) for i in range(count)])
        for step in range(1, count)
    ]


def ring_halves(low, high, axis):
    up = [(i, (i + 1) % 4) for i in range(4)]
    down = [(i, (i + 3) % 4) for i in range(4)]
    low_behind = lax.ppermute(low, axis, up)
    high_ahead = lax.ppermute(high, axis, down)
    high_behind = lax.ppermute(high, axis, up)
    low_ahead = lax.ppermute(low, axis, down)
    low_across = lax.ppermute(low_behind, axis, up)
    high_across = lax.ppermute(high_ahead, axis, down)
    return (low_behind, high_behind), (low_ahead, high_ahead), (low_across, high_across)


def swap(value):
    return lax.ppermute(value, "core", [(0, 1), (1, 0)])


def pick(value, index):
    return lax.dynamic_index_in_dim(value, index, 0, keepdims=False)


def dot_nt(a, b):
    return lax.dot_general(a, b, (((1,), (1,)), ((), ())), preferred_element_type=F32)


def in_vmem(kernel, out_shape, flops, args):
    return pl.pallas_call(
        kernel,
        in_specs=[pl.BlockSpec(memory_space=pltpu.VMEM)] * len(args),
        out_specs=pl.BlockSpec(memory_space=pltpu.VMEM),
        out_shape=jax.ShapeDtypeStruct(out_shape, BF),
        compiler_params=pltpu.CompilerParams(vmem_limit_bytes=24 * 1024 * 1024),
        cost_estimate=pl.CostEstimate(
            flops=flops, bytes_accessed=sum(a.size * 2 for a in args), transcendentals=0
        ),
    )(*args)


def prepare_kernel(hid_ref, emb_ref, token_ref, hid_out, emb_out):
    row = lax.broadcasted_iota(jnp.int32, (256, 256), 0)
    col = lax.broadcasted_iota(jnp.int32, (256, 256), 1)
    within = col % 128
    chosen = (row == (within // 4) * 8 + within % 4 + 4 * (col // 128)).astype(BF)
    split = jnp.dot(hid_ref[...], chosen, preferred_element_type=F32).astype(BF)
    hid_out[0] = split[:, :128]
    hid_out[1] = split[:, 128:]
    low_codes = lax.broadcasted_iota(jnp.int32, (128, 1024), 0)
    for core in range(C):
        index = 1 - core
        token = token_ref[index : index + 1]
        low = (low_codes == token % 128).astype(BF)
        high = token // 128
        table = jnp.concatenate(
            [emb_ref[index, :, h * 128 : (h + 1) * 128] for h in range(16)], axis=0
        )
        found = jnp.dot(table, low, preferred_element_type=F32)
        total = jnp.zeros((16, 1024), F32)
        for h in range(16):
            total += jnp.where(high == h, found[h * 16 : (h + 1) * 16], 0.0)
        for z in range(Z):
            emb_out[z, core] = jnp.concatenate(
                [total[:, x * 256 + z * 32 : x * 256 + z * 32 + 32] for x in range(X)], axis=1
            ).astype(BF)


def prepare(hid_t, emb_t, token):
    return pl.pallas_call(
        prepare_kernel,
        in_specs=[pl.BlockSpec(memory_space=pltpu.VMEM)] * 3,
        out_specs=[pl.BlockSpec(memory_space=pltpu.VMEM)] * 2,
        out_shape=[
            jax.ShapeDtypeStruct((C, 64, 128), BF),
            jax.ShapeDtypeStruct((Z, C, 16, 128), BF),
        ],
        compiler_params=pltpu.CompilerParams(vmem_limit_bytes=24 * 1024 * 1024),
    )(hid_t, emb_t, token)


def qkv_kernel(*refs):
    part_refs, (own_ref, oth_ref, hid_ref, out_ref) = refs[:8], refs[8:]
    yi, ci = lax.axis_index("y"), lax.axis_index("core")
    squares = jnp.zeros((1, 128), F32)
    sums = [jnp.zeros((192, 128), F32), jnp.zeros((192, 128), F32)]
    for index, step in enumerate((0, 3, 1, 2)):
        at = lax.rem(yi + step, Y)
        gains = part_refs[2 * index][512:528].astype(F32)
        for z in range(Z):
            rows = pl.ds((z % 4) * 128, 128)
            block = part_refs[2 * index + z // 4][rows]
            wide = block.astype(F32)
            squares += jnp.sum(wide * wide, axis=0, keepdims=True)
            columns = pl.ds(pl.multiple_of(z * 512 + at * 128, 128), 128)
            for which, w_ref in enumerate((own_ref, oth_ref)):
                w = (w_ref[:, columns].astype(F32) * gains[z : z + 1]).astype(BF)
                sums[which] += jnp.dot(w, block, preferred_element_type=F32)
    inv = lax.rsqrt(squares / D + eps)
    own, oth = sums[0] * inv, sums[1] * inv
    low = jnp.where(ci == 0, own, oth)
    high = jnp.where(ci == 0, oth, own)
    pieces = []
    for i in range(3):
        pieces += [low[i * 64 : (i + 1) * 64], high[i * 64 : (i + 1) * 64]]
    pieces.append(hid_ref[...].astype(F32))
    out_ref[...] = jnp.concatenate(pieces, axis=0).T.astype(BF)


def project_kernel(moved_ref, w_ref, out_ref):
    acc = jnp.zeros((128, DD), F32)
    for i in range(4):
        acc += jnp.dot(
            moved_ref[:, i * 128 : (i + 1) * 128],
            w_ref[2 * i : 2 * i + 2, 128:].reshape(128, DD),
            preferred_element_type=F32,
        )
    for block in range(8):
        low = acc[:, block * 64 : (block + 1) * 64]
        high = acc[:, 512 + block * 64 : 512 + (block + 1) * 64]
        out_ref[block] = jnp.concatenate([low, high], axis=1).astype(BF)


def depth_in_kernel(own_ref, oth_ref, w_ref, emb_ref, out_ref):
    acc = emb_ref[...].astype(F32)
    for i in range(X):
        w = w_ref[2 * i : 2 * i + 2, :128]
        acc += jnp.dot(own_ref[i], w[:, :64].reshape(128, DD), preferred_element_type=F32)
        acc += jnp.dot(oth_ref[i], w[:, 64:].reshape(128, DD), preferred_element_type=F32)
    out_ref[...] = acc.astype(BF)


def depth_ff_kernel(a_ref, b_ref, c_ref, d_ref, gain_ref, w_ref, out_ref):
    x = a_ref[...].astype(F32) + b_ref[...].astype(F32)
    x = x + c_ref[...].astype(F32) + d_ref[...].astype(F32)
    mean = jnp.sum(x * x, axis=1, keepdims=True) / DD
    xn = (x * lax.rsqrt(mean + eps) * gain_ref[...]).astype(BF)
    acc = x * (1.0 / Y)
    wide = 2 * HID_PAD
    for i in range(4):
        w = w_ref.at[2 * i : 2 * i + 2]
        gate = dot_nt(xn, w[:, :wide].reshape(2 * wide, DD))
        upper = dot_nt(xn, w[:, wide : 2 * wide].reshape(2 * wide, DD))
        act = (jax.nn.silu(gate) * upper).astype(BF)
        acc += jnp.dot(
            act, w[:, 2 * wide :].reshape(2 * wide, DD), preferred_element_type=F32
        )
    for block in range(Z):
        turned = acc[:, block * 128 : (block + 1) * 128].T
        out_ref[block] = turned.reshape(Y, 32, 128).astype(BF)


def per_device(
    hidden_in,
    norm_gain,
    w_qkv,
    w_out,
    cache_keys,
    cache_values,
    lengths,
    tokens,
    w_in,
    embed,
    depth_gain,
    w_gate_up,
    w_down,
):
    xi, zi, yi, ci = (lax.axis_index(a) for a in ("cb", "z", "y", "core"))
    other = 1 - ci

    with jax.named_scope("gather_hidden"):
        hid_split, emb_sent = prepare(hidden_in.T, embed.transpose(0, 2, 1), tokens.T)
        gain_row = jnp.pad(norm_gain[None, :], ((0, 7), (0, 64)))
        copies = jnp.concatenate(
            [
                jnp.broadcast_to(hid_split[None], (Z, C, 64, 128)),
                jnp.broadcast_to(gain_row, (Z, C, 8, 128)),
                emb_sent,
            ],
            axis=2,
        )
        column = exchange(copies.reshape(16, 88, 128), ("z", "core")).reshape(Z, C, 88, 128)
        emb_here = column[:, :, 72:]
        started = swap(hid_split[0, :16])
        w_in, w_out, w_gate_up, w_down, w_qkv, started = lax.optimization_barrier(
            (w_in, w_out, w_gate_up, w_down, w_qkv, started)
        )

    with jax.named_scope("pack_weights"):
        recv_a = swap(pick(w_in, other))
        wo = lax.dynamic_slice_in_dim(w_out, xi * DD, DD, 1)
        first_in = jnp.concatenate([pick(w_in, ci), recv_a, wo], axis=0)
        gu_t = w_gate_up.transpose(0, 3, 1, 2)
        gap = ((0, HID_PAD - HID), (0, 0))

        def stacked(step):
            gu = pick(gu_t, step)
            parts = (gu[:, 0], gu[:, 1], pick(w_down, step))
            return [jnp.pad(part, gap) for part in parts]

        recv_b = swap(jnp.concatenate(stacked(other), axis=0))
        second_in = []
        for index, part in enumerate(stacked(ci)):
            second_in += [part, recv_b[index * HID_PAD : (index + 1) * HID_PAD]]
        second_in = jnp.concatenate(second_in, axis=0)
        first = lax.all_gather(first_in, "z")
        second = lax.all_gather(second_in, "z")

    with jax.named_scope("norm"):
        w_own = w_qkv.transpose(0, 2, 1).reshape(192, D)
        w_oth = swap(w_own)
        gains = jnp.pad(column[:, :, 64, :64].reshape(Z, 128), ((0, 8), (0, 0)))
        low = jnp.concatenate([column[:4, :, :64].reshape(512, 128), gains], axis=0)
        high = column[4:, :, :64].reshape(512, 128)
        others = ring_halves(low, high, "y")

    with jax.named_scope("qkv"):
        hid_cols = pick(column, zi)[:, :64].reshape(128, 128)
        sent = in_vmem(
            qkv_kernel,
            (128, 512),
            2 * 128 * 384 * D,
            (low, high, *others[0], *others[1], *others[2], w_own, w_oth, hid_cols),
        )
        got = exchange(sent.reshape(32, 4, 512), ("z", "y"))
        got = got.reshape(HEADS, 4, 4, HEAD_DIM).transpose(1, 2, 0, 3)

    with jax.named_scope("embed"):
        moved_emb = lax.ppermute(
            emb_here, ("cb", "core"), [(2 * x, 2 * ((x + 1) % X)) for x in range(X)]
        )
        emb = jnp.where(ci == 0, moved_emb, emb_here).reshape(256, 128)
        source = lax.broadcasted_iota(jnp.int32, (256, DD), 0)
        target = lax.broadcasted_iota(jnp.int32, (256, DD), 1)
        place = (target == (source // 32) * 128 + yi * 32 + source % 32).astype(BF)
        emb = jnp.dot(emb.T, place, preferred_element_type=F32).astype(BF)

    with jax.named_scope("attend"):
        got, first = lax.optimization_barrier((got, first))
        query_h, key_new, value_new = got[:, 0], got[:, 1], got[:, 2]
        hid_rows = got[:, 3]
        scale = 1.0 / math.sqrt(HEAD_DIM)
        keys_h = cache_keys.reshape(4, CACHE, HEADS, HEAD_DIM)
        values_h = cache_values.reshape(4, CACHE, HEADS, HEAD_DIM)
        scores = jnp.einsum("rhe,rphe->rhp", query_h, keys_h, preferred_element_type=F32) * scale
        live = lax.broadcasted_iota(jnp.int32, (1, 1, CACHE), 2) < lengths[:, None, None]
        scores = jnp.where(live, scores, -1e30)
        fresh = jnp.sum(query_h.astype(F32) * key_new.astype(F32), axis=-1) * scale
        top = jnp.maximum(jnp.max(scores, axis=-1), fresh)
        weights = jnp.exp(scores - top[..., None])
        weight_new = jnp.exp(fresh - top)
        total = jnp.sum(weights, axis=-1) + weight_new
        probs = (weights / total[..., None]).astype(BF)
        prob_new = (weight_new / total).astype(BF)
        mixed = jnp.einsum("rhp,rphe->rhe", probs, values_h, preferred_element_type=F32)
        mixed = mixed + prob_new.astype(F32)[..., None] * value_new.astype(F32)
        attended = mixed.astype(BF)

    with jax.named_scope("project"):
        att = attended.reshape(4, Z, Y, C, 64).transpose(2, 3, 0, 1, 4).reshape(1, 8, 4, 512)
        att = jnp.broadcast_to(att, (X, 8, 4, 512))
        res = hid_rows.reshape(4, X, 2, Y, C, 64).transpose(1, 3, 4, 0, 2, 5)
        res = res.reshape(X, 8, 4, 128)
        moved = exchange(
            jnp.concatenate([att, res], axis=-1).reshape(32, 4, 640), ("cb", "y", "core")
        ).reshape(128, 640)
        part = in_vmem(project_kernel, (8, 128, 128), 2 * 128 * 512 * DD, (moved[:, :512], first))
        part = exchange(part, ("y", "core"))
        temporal = jnp.sum(part.astype(F32), axis=0) + moved[:, 512:].astype(F32)
        temporal = temporal.astype(BF)
        around = from_each(temporal, "cb")
        frame = jnp.zeros((X, 128, 128), BF)
        for step, piece in enumerate(around):
            at = lax.rem(xi - step + X, X)
            frame = lax.dynamic_update_slice(frame, piece[None], (at, 0, 0))
        frame_oth = swap(frame)

    with jax.named_scope("depth"):
        x_part = in_vmem(
            depth_in_kernel, (128, DD), 2 * 128 * 1024 * DD, (frame, frame_oth, first, emb)
        )
        rows = lax.dynamic_slice_in_dim(frame, xi * 32, 32, 1)
        rows = rows.reshape(X, 2, 16, 2, 64).transpose(0, 3, 2, 1, 4).reshape(Z, 16, 128)
        rows, second = lax.optimization_barrier((rows, second))
        gain_d = lax.dynamic_slice_in_dim(depth_gain, ci, 1, 0).astype(F32)
        out = in_vmem(
            depth_ff_kernel,
            (Z, Y, 32, 128),
            6 * 128 * 768 * DD,
            (*from_each(x_part, "y"), gain_d, second),
        )
        out = exchange(out.reshape(64, 16, 128), TP).reshape(Z, Y, C, 16, 128)
        out = jnp.sum(out.astype(F32), axis=1).astype(BF)

    with jax.named_scope("place_outputs"):
        depth_out = out.reshape(Z, C, 16, X, 32).transpose(1, 3, 0, 4, 2)
        depth_out = depth_out.reshape(C, 1024, 16)
        rows = exchange(rows, "z")
        temporal_out = rows.reshape(Z, 16, 2, 64).transpose(0, 2, 1, 3).reshape(256, 64)
    return (temporal_out, depth_out)


def solution(mesh):
    fine = Mesh(mesh.devices.reshape(X, Z, Y, C), ("cb", "z", "y", "core"))
    every = ("cb",) + TP
    in_specs = (
        P("cb", TP),
        P(TP),
        P(None, None, TP),
        P(TP, None),
        P(every, None, None),
        P(every, None, None),
        P(every),
        P(None, "cb"),
        P("cb", TP, None),
        P("cb", None, TP),
        P("cb", None),
        P("cb", None, None, TP),
        P("cb", TP, None),
    )
    out_specs = (P("cb", TP), P("cb", None, TP))
    return jax.shard_map(
        per_device, mesh=fine, in_specs=in_specs, out_specs=out_specs, check_vma=False
    )
```

```python
import math

import jax
import jax.numpy as jnp
from jax import lax
from jax.experimental import pallas as pl
from jax.experimental.pallas import tpu as pltpu
from jax.sharding import Mesh, PartitionSpec as P

D = 4096
HEADS = 32
HEAD_DIM = 128
DD = 1024
CARD = 2048
CACHE = 64
X, Z, Y, C = 4, 8, 4, 2
HID = 44
HID_PAD = 48

eps = 1e-05
BF = jnp.bfloat16
F32 = jnp.float32
TP = ("z", "y", "core")


def exchange(value, axis):
    return lax.all_to_all(value, axis, split_axis=0, concat_axis=0, tiled=True)


def spread(value, axis):
    count = lax.axis_size(axis)
    copies = jnp.broadcast_to(value[None], (count,) + value.shape)
    return exchange(copies, axis)


def from_each(value, axis):
    count = lax.axis_size(axis)
    return [value] + [
        lax.ppermute(value, axis, [(i, (i + step) % count) for i in range(count)])
        for step in range(1, count)
    ]


def ring_halves(low, high, axis):
    up = [(i, (i + 1) % 4) for i in range(4)]
    down = [(i, (i + 3) % 4) for i in range(4)]
    low_behind = lax.ppermute(low, axis, up)
    high_ahead = lax.ppermute(high, axis, down)
    high_behind = lax.ppermute(high, axis, up)
    low_ahead = lax.ppermute(low, axis, down)
    low_across = lax.ppermute(low_behind, axis, up)
    high_across = lax.ppermute(high_ahead, axis, down)
    return (low_behind, high_behind), (low_ahead, high_ahead), (low_across, high_across)


def swap(value):
    return lax.ppermute(value, "core", [(0, 1), (1, 0)])


def pick(value, index):
    return lax.dynamic_index_in_dim(value, index, 0, keepdims=False)


def dot_nt(a, b):
    return lax.dot_general(a, b, (((1,), (1,)), ((), ())), preferred_element_type=F32)


def in_vmem(kernel, out_shape, flops, args):
    return pl.pallas_call(
        kernel,
        in_specs=[pl.BlockSpec(memory_space=pltpu.VMEM)] * len(args),
        out_specs=pl.BlockSpec(memory_space=pltpu.VMEM),
        out_shape=jax.ShapeDtypeStruct(out_shape, BF),
        compiler_params=pltpu.CompilerParams(vmem_limit_bytes=24 * 1024 * 1024),
        cost_estimate=pl.CostEstimate(
            flops=flops, bytes_accessed=sum(a.size * 2 for a in args), transcendentals=0
        ),
    )(*args)


def prepare_kernel(hid_ref, emb_ref, token_ref, hid_out, emb_out):
    row = lax.broadcasted_iota(jnp.int32, (256, 256), 0)
    col = lax.broadcasted_iota(jnp.int32, (256, 256), 1)
    within = col % 128
    chosen = (row == (within // 4) * 8 + within % 4 + 4 * (col // 128)).astype(BF)
    split = jnp.dot(hid_ref[...], chosen, preferred_element_type=F32).astype(BF)
    hid_out[0] = split[:, :128]
    hid_out[1] = split[:, 128:]
    low_codes = lax.broadcasted_iota(jnp.int32, (128, 1024), 0)
    for core in range(C):
        index = 1 - core
        token = token_ref[index : index + 1]
        low = (low_codes == token % 128).astype(BF)
        high = token // 128
        table = jnp.concatenate(
            [emb_ref[index, :, h * 128 : (h + 1) * 128] for h in range(16)], axis=0
        )
        found = jnp.dot(table, low, preferred_element_type=F32)
        total = jnp.zeros((16, 1024), F32)
        for h in range(16):
            total += jnp.where(high == h, found[h * 16 : (h + 1) * 16], 0.0)
        for z in range(Z):
            emb_out[z, core] = jnp.concatenate(
                [total[:, x * 256 + z * 32 : x * 256 + z * 32 + 32] for x in range(X)], axis=1
            ).astype(BF)


def prepare(hid_t, emb_t, token):
    return pl.pallas_call(
        prepare_kernel,
        in_specs=[pl.BlockSpec(memory_space=pltpu.VMEM)] * 3,
        out_specs=[pl.BlockSpec(memory_space=pltpu.VMEM)] * 2,
        out_shape=[
            jax.ShapeDtypeStruct((C, 64, 128), BF),
            jax.ShapeDtypeStruct((Z, C, 16, 128), BF),
        ],
        compiler_params=pltpu.CompilerParams(vmem_limit_bytes=24 * 1024 * 1024),
    )(hid_t, emb_t, token)


def qkv_kernel(*refs):
    part_refs, (own_ref, oth_ref, hid_ref, out_ref) = refs[:8], refs[8:]
    yi, ci = lax.axis_index("y"), lax.axis_index("core")
    squares = jnp.zeros((1, 128), F32)
    sums = [jnp.zeros((192, 128), F32), jnp.zeros((192, 128), F32)]
    for index, step in enumerate((0, 3, 1, 2)):
        at = lax.rem(yi + step, Y)
        gains = part_refs[2 * index][512:528].astype(F32)
        for z in range(Z):
            rows = pl.ds((z % 4) * 128, 128)
            block = part_refs[2 * index + z // 4][rows]
            wide = block.astype(F32)
            squares += jnp.sum(wide * wide, axis=0, keepdims=True)
            columns = pl.ds(pl.multiple_of(z * 512 + at * 128, 128), 128)
            for which, w_ref in enumerate((own_ref, oth_ref)):
                w = (w_ref[:, columns].astype(F32) * gains[z : z + 1]).astype(BF)
                sums[which] += jnp.dot(w, block, preferred_element_type=F32)
    inv = lax.rsqrt(squares / D + eps)
    own, oth = sums[0] * inv, sums[1] * inv
    low = jnp.where(ci == 0, own, oth)
    high = jnp.where(ci == 0, oth, own)
    pieces = []
    for i in range(3):
        pieces += [low[i * 64 : (i + 1) * 64], high[i * 64 : (i + 1) * 64]]
    pieces.append(hid_ref[...].astype(F32))
    out_ref[...] = jnp.concatenate(pieces, axis=0).T.astype(BF)


def project_kernel(moved_ref, w_ref, out_ref):
    acc = jnp.zeros((128, DD), F32)
    for i in range(4):
        acc += jnp.dot(
            moved_ref[:, i * 128 : (i + 1) * 128],
            w_ref[2 * i : 2 * i + 2, 128:].reshape(128, DD),
            preferred_element_type=F32,
        )
    for block in range(8):
        low = acc[:, block * 64 : (block + 1) * 64]
        high = acc[:, 512 + block * 64 : 512 + (block + 1) * 64]
        out_ref[block] = jnp.concatenate([low, high], axis=1).astype(BF)


def depth_in_kernel(own_ref, oth_ref, w_ref, emb_ref, out_ref):
    acc = emb_ref[...].astype(F32)
    for i in range(X):
        w = w_ref[2 * i : 2 * i + 2, :128]
        acc += jnp.dot(own_ref[i], w[:, :64].reshape(128, DD), preferred_element_type=F32)
        acc += jnp.dot(oth_ref[i], w[:, 64:].reshape(128, DD), preferred_element_type=F32)
    out_ref[...] = acc.astype(BF)


def depth_ff_kernel(a_ref, b_ref, c_ref, d_ref, gain_ref, w_ref, out_ref):
    x = a_ref[...].astype(F32) + b_ref[...].astype(F32)
    x = x + c_ref[...].astype(F32) + d_ref[...].astype(F32)
    mean = jnp.sum(x * x, axis=1, keepdims=True) / DD
    xn = (x * lax.rsqrt(mean + eps) * gain_ref[...]).astype(BF)
    acc = x * (1.0 / Y)
    wide = 2 * HID_PAD
    for i in range(4):
        w = w_ref.at[2 * i : 2 * i + 2]
        gate = dot_nt(xn, w[:, :wide].reshape(2 * wide, DD))
        upper = dot_nt(xn, w[:, wide : 2 * wide].reshape(2 * wide, DD))
        act = (jax.nn.silu(gate) * upper).astype(BF)
        acc += jnp.dot(
            act, w[:, 2 * wide :].reshape(2 * wide, DD), preferred_element_type=F32
        )
    for block in range(Z):
        turned = acc[:, block * 128 : (block + 1) * 128].T
        out_ref[block] = turned.reshape(Y, 32, 128).astype(BF)


def per_device(
    hidden_in,
    norm_gain,
    w_qkv,
    w_out,
    cache_keys,
    cache_values,
    lengths,
    tokens,
    w_in,
    embed,
    depth_gain,
    w_gate_up,
    w_down,
):
    xi, zi, yi, ci = (lax.axis_index(a) for a in ("cb", "z", "y", "core"))
    other = 1 - ci

    with jax.named_scope("gather_hidden"):
        hid_split, emb_sent = prepare(hidden_in.T, embed.transpose(0, 2, 1), tokens.T)
        gain_row = jnp.pad(norm_gain[None, :], ((0, 7), (0, 64)))
        copies = jnp.concatenate(
            [
                jnp.broadcast_to(hid_split[None], (Z, C, 64, 128)),
                jnp.broadcast_to(gain_row, (Z, C, 8, 128)),
                emb_sent,
            ],
            axis=2,
        )
        column = exchange(copies.reshape(16, 88, 128), ("z", "core")).reshape(Z, C, 88, 128)
        emb_here = column[:, :, 72:]
        started = swap(hid_split[0, :16])
        w_in, w_out, w_gate_up, w_down, w_qkv, started = lax.optimization_barrier(
            (w_in, w_out, w_gate_up, w_down, w_qkv, started)
        )

    with jax.named_scope("pack_weights"):
        recv_a = swap(pick(w_in, other))
        wo = lax.dynamic_slice_in_dim(w_out, xi * DD, DD, 1)
        first_in = jnp.concatenate([pick(w_in, ci), recv_a, wo], axis=0)
        gu_t = w_gate_up.transpose(0, 3, 1, 2)
        gap = ((0, HID_PAD - HID), (0, 0))

        def stacked(step):
            gu = pick(gu_t, step)
            parts = (gu[:, 0], gu[:, 1], pick(w_down, step))
            return [jnp.pad(part, gap) for part in parts]

        recv_b = swap(jnp.concatenate(stacked(other), axis=0))
        second_in = []
        for index, part in enumerate(stacked(ci)):
            second_in += [part, recv_b[index * HID_PAD : (index + 1) * HID_PAD]]
        second_in = jnp.concatenate(second_in, axis=0)
        first = lax.all_gather(first_in, "z")
        second = lax.all_gather(second_in, "z")

    with jax.named_scope("norm"):
        w_own = w_qkv.transpose(0, 2, 1).reshape(192, D)
        w_oth = swap(w_own)
        gains = jnp.pad(column[:, :, 64, :64].reshape(Z, 128), ((0, 8), (0, 0)))
        low = jnp.concatenate([column[:4, :, :64].reshape(512, 128), gains], axis=0)
        high = column[4:, :, :64].reshape(512, 128)
        others = ring_halves(low, high, "y")

    with jax.named_scope("qkv"):
        hid_cols = pick(column, zi)[:, :64].reshape(128, 128)
        sent = in_vmem(
            qkv_kernel,
            (128, 512),
            2 * 128 * 384 * D,
            (low, high, *others[0], *others[1], *others[2], w_own, w_oth, hid_cols),
        )
        got = exchange(sent.reshape(32, 4, 512), ("z", "y"))
        got = got.reshape(HEADS, 4, 4, HEAD_DIM).transpose(1, 2, 0, 3)

    with jax.named_scope("embed"):
        pairs = [(2 * x, 2 * ((x + 1) % X)) for x in range(X)]
        pairs += [(2 * x + 1, 2 * x + 1) for x in range(X)]
        emb = lax.ppermute(emb_here, ("cb", "core"), pairs).reshape(256, 128)
        source = lax.broadcasted_iota(jnp.int32, (256, DD), 0)
        target = lax.broadcasted_iota(jnp.int32, (256, DD), 1)
        place = (target == (source // 32) * 128 + yi * 32 + source % 32).astype(BF)
        emb = jnp.dot(emb.T, place, preferred_element_type=F32).astype(BF)

    with jax.named_scope("attend"):
        got, first = lax.optimization_barrier((got, first))
        query_h, key_new, value_new = got[:, 0], got[:, 1], got[:, 2]
        hid_rows = got[:, 3]
        scale = 1.0 / math.sqrt(HEAD_DIM)
        keys_h = cache_keys.reshape(4, CACHE, HEADS, HEAD_DIM)
        values_h = cache_values.reshape(4, CACHE, HEADS, HEAD_DIM)
        scores = jnp.einsum("rhe,rphe->rhp", query_h, keys_h, preferred_element_type=F32) * scale
        live = lax.broadcasted_iota(jnp.int32, (1, 1, CACHE), 2) < lengths[:, None, None]
        scores = jnp.where(live, scores, -1e30)
        fresh = jnp.sum(query_h.astype(F32) * key_new.astype(F32), axis=-1) * scale
        top = jnp.maximum(jnp.max(scores, axis=-1), fresh)
        weights = jnp.exp(scores - top[..., None])
        weight_new = jnp.exp(fresh - top)
        total = jnp.sum(weights, axis=-1) + weight_new
        probs = (weights / total[..., None]).astype(BF)
        prob_new = (weight_new / total).astype(BF)
        mixed = jnp.einsum("rhp,rphe->rhe", probs, values_h, preferred_element_type=F32)
        mixed = mixed + prob_new.astype(F32)[..., None] * value_new.astype(F32)
        attended = mixed.astype(BF)

    with jax.named_scope("project"):
        att = attended.reshape(4, Z, Y, C, 64).transpose(2, 3, 0, 1, 4).reshape(1, 8, 4, 512)
        att = jnp.broadcast_to(att, (X, 8, 4, 512))
        res = hid_rows.reshape(4, X, 2, Y, C, 64).transpose(1, 3, 4, 0, 2, 5)
        res = res.reshape(X, 8, 4, 128)
        moved = exchange(
            jnp.concatenate([att, res], axis=-1).reshape(32, 4, 640), ("cb", "y", "core")
        ).reshape(128, 640)
        part = in_vmem(project_kernel, (8, 128, 128), 2 * 128 * 512 * DD, (moved[:, :512], first))
        part = exchange(part, ("y", "core"))
        temporal = jnp.sum(part.astype(F32), axis=0) + moved[:, 512:].astype(F32)
        temporal = temporal.astype(BF)
        around = from_each(temporal, "cb")
        frame = jnp.zeros((X, 128, 128), BF)
        for step, piece in enumerate(around):
            at = lax.rem(xi - step + X, X)
            frame = lax.dynamic_update_slice(frame, piece[None], (at, 0, 0))
        frame_oth = swap(frame)

    with jax.named_scope("depth"):
        x_part = in_vmem(
            depth_in_kernel, (128, DD), 2 * 128 * 1024 * DD, (frame, frame_oth, first, emb)
        )
        rows = lax.dynamic_slice_in_dim(frame, xi * 32, 32, 1)
        rows = rows.reshape(X, 2, 16, 2, 64).transpose(0, 3, 2, 1, 4).reshape(Z, 16, 128)
        rows, second = lax.optimization_barrier((rows, second))
        gain_d = lax.dynamic_slice_in_dim(depth_gain, ci, 1, 0).astype(F32)
        out = in_vmem(
            depth_ff_kernel,
            (Z, Y, 32, 128),
            6 * 128 * 768 * DD,
            (*from_each(x_part, "y"), gain_d, second),
        )
        out = exchange(out.reshape(64, 16, 128), TP).reshape(Z, Y, C, 16, 128)
        out = jnp.sum(out.astype(F32), axis=1).astype(BF)

    with jax.named_scope("place_outputs"):
        depth_out = out.reshape(Z, C, 16, X, 32).transpose(1, 3, 0, 4, 2)
        depth_out = depth_out.reshape(C, 1024, 16)
        rows = exchange(rows, "z")
        temporal_out = rows.reshape(Z, 16, 2, 64).transpose(0, 2, 1, 3).reshape(256, 64)
    return (temporal_out, depth_out)


def solution(mesh):
    fine = Mesh(mesh.devices.reshape(X, Z, Y, C), ("cb", "z", "y", "core"))
    every = ("cb",) + TP
    in_specs = (
        P("cb", TP),
        P(TP),
        P(None, None, TP),
        P(TP, None),
        P(every, None, None),
        P(every, None, None),
        P(every),
        P(None, "cb"),
        P("cb", TP, None),
        P("cb", None, TP),
        P("cb", None),
        P("cb", None, None, TP),
        P("cb", TP, None),
    )
    out_specs = (P("cb", TP), P("cb", None, TP))
    return jax.shard_map(
        per_device, mesh=fine, in_specs=in_specs, out_specs=out_specs, check_vma=False
    )
```

```python
import math

import jax
import jax.numpy as jnp
from jax import lax
from jax.experimental import pallas as pl
from jax.experimental.pallas import tpu as pltpu
from jax.sharding import Mesh, PartitionSpec as P

D = 4096
HEADS = 32
HEAD_DIM = 128
DD = 1024
CARD = 2048
CACHE = 64
X, Z, Y, C = 4, 8, 4, 2
HID = 44
HID_PAD = 48

eps = 1e-05
BF = jnp.bfloat16
F32 = jnp.float32
TP = ("z", "y", "core")


def exchange(value, axis):
    return lax.all_to_all(value, axis, split_axis=0, concat_axis=0, tiled=True)


def spread(value, axis):
    count = lax.axis_size(axis)
    copies = jnp.broadcast_to(value[None], (count,) + value.shape)
    return exchange(copies, axis)


def from_each(value, axis):
    count = lax.axis_size(axis)
    return [value] + [
        lax.ppermute(value, axis, [(i, (i + step) % count) for i in range(count)])
        for step in range(1, count)
    ]


def ring_halves(low, high, axis):
    up = [(i, (i + 1) % 4) for i in range(4)]
    down = [(i, (i + 3) % 4) for i in range(4)]
    low_behind = lax.ppermute(low, axis, up)
    high_ahead = lax.ppermute(high, axis, down)
    high_behind = lax.ppermute(high, axis, up)
    low_ahead = lax.ppermute(low, axis, down)
    low_across = lax.ppermute(low_behind, axis, up)
    high_across = lax.ppermute(high_ahead, axis, down)
    return (low_behind, high_behind), (low_ahead, high_ahead), (low_across, high_across)


def swap(value):
    return lax.ppermute(value, "core", [(0, 1), (1, 0)])


def pick(value, index):
    return lax.dynamic_index_in_dim(value, index, 0, keepdims=False)


def dot_nt(a, b):
    return lax.dot_general(a, b, (((1,), (1,)), ((), ())), preferred_element_type=F32)


def in_vmem(kernel, out_shape, flops, args):
    return pl.pallas_call(
        kernel,
        in_specs=[pl.BlockSpec(memory_space=pltpu.VMEM)] * len(args),
        out_specs=pl.BlockSpec(memory_space=pltpu.VMEM),
        out_shape=jax.ShapeDtypeStruct(out_shape, BF),
        compiler_params=pltpu.CompilerParams(vmem_limit_bytes=24 * 1024 * 1024),
        cost_estimate=pl.CostEstimate(
            flops=flops, bytes_accessed=sum(a.size * 2 for a in args), transcendentals=0
        ),
    )(*args)


def prepare_kernel(hid_ref, emb_ref, token_ref, hid_out, emb_out):
    row = lax.broadcasted_iota(jnp.int32, (256, 256), 0)
    col = lax.broadcasted_iota(jnp.int32, (256, 256), 1)
    within = col % 128
    chosen = (row == (within // 4) * 8 + within % 4 + 4 * (col // 128)).astype(BF)
    split = jnp.dot(hid_ref[...], chosen, preferred_element_type=F32).astype(BF)
    hid_out[0] = split[:, :128]
    hid_out[1] = split[:, 128:]
    low_codes = lax.broadcasted_iota(jnp.int32, (128, 1024), 0)
    for core in range(C):
        index = 1 - core
        token = token_ref[index : index + 1]
        low = (low_codes == token % 128).astype(BF)
        high = token // 128
        table = jnp.concatenate(
            [emb_ref[index, :, h * 128 : (h + 1) * 128] for h in range(16)], axis=0
        )
        found = jnp.dot(table, low, preferred_element_type=F32)
        total = jnp.zeros((16, 1024), F32)
        for h in range(16):
            total += jnp.where(high == h, found[h * 16 : (h + 1) * 16], 0.0)
        for z in range(Z):
            emb_out[z, core] = jnp.concatenate(
                [total[:, x * 256 + z * 32 : x * 256 + z * 32 + 32] for x in range(X)], axis=1
            ).astype(BF)


def prepare(hid_t, emb_t, token):
    return pl.pallas_call(
        prepare_kernel,
        in_specs=[pl.BlockSpec(memory_space=pltpu.VMEM)] * 3,
        out_specs=[pl.BlockSpec(memory_space=pltpu.VMEM)] * 2,
        out_shape=[
            jax.ShapeDtypeStruct((C, 64, 128), BF),
            jax.ShapeDtypeStruct((Z, C, 16, 128), BF),
        ],
        compiler_params=pltpu.CompilerParams(vmem_limit_bytes=24 * 1024 * 1024),
    )(hid_t, emb_t, token)


def qkv_kernel(*refs):
    part_refs, (own_ref, oth_ref, hid_ref, out_ref) = refs[:8], refs[8:]
    yi, ci = lax.axis_index("y"), lax.axis_index("core")
    squares = jnp.zeros((1, 128), F32)
    sums = [jnp.zeros((192, 128), F32), jnp.zeros((192, 128), F32)]
    for index, step in enumerate((0, 3, 1, 2)):
        at = lax.rem(yi + step, Y)
        gains = part_refs[2 * index][512:528].astype(F32)
        for z in range(Z):
            rows = pl.ds((z % 4) * 128, 128)
            block = part_refs[2 * index + z // 4][rows]
            wide = block.astype(F32)
            squares += jnp.sum(wide * wide, axis=0, keepdims=True)
            columns = pl.ds(pl.multiple_of(z * 512 + at * 128, 128), 128)
            for which, w_ref in enumerate((own_ref, oth_ref)):
                w = (w_ref[:, columns].astype(F32) * gains[z : z + 1]).astype(BF)
                sums[which] += jnp.dot(w, block, preferred_element_type=F32)
    inv = lax.rsqrt(squares / D + eps)
    own, oth = sums[0] * inv, sums[1] * inv
    low = jnp.where(ci == 0, own, oth)
    high = jnp.where(ci == 0, oth, own)
    pieces = []
    for i in range(3):
        pieces += [low[i * 64 : (i + 1) * 64], high[i * 64 : (i + 1) * 64]]
    pieces.append(hid_ref[...].astype(F32))
    out_ref[...] = jnp.concatenate(pieces, axis=0).T.astype(BF)


def project_kernel(moved_ref, w_ref, out_ref):
    acc = jnp.zeros((128, DD), F32)
    for i in range(4):
        acc += jnp.dot(
            moved_ref[:, i * 128 : (i + 1) * 128],
            w_ref[2 * i : 2 * i + 2].reshape(128, DD),
            preferred_element_type=F32,
        )
    for block in range(8):
        low = acc[:, block * 64 : (block + 1) * 64]
        high = acc[:, 512 + block * 64 : 512 + (block + 1) * 64]
        out_ref[block] = jnp.concatenate([low, high], axis=1).astype(BF)


def depth_in_kernel(own_ref, oth_ref, w_ref, emb_ref, out_ref):
    acc = emb_ref[...].astype(F32)
    for i in range(X):
        w = w_ref[2 * i : 2 * i + 2, :128]
        acc += jnp.dot(own_ref[i], w[:, :64].reshape(128, DD), preferred_element_type=F32)
        acc += jnp.dot(oth_ref[i], w[:, 64:].reshape(128, DD), preferred_element_type=F32)
    out_ref[...] = acc.astype(BF)


def depth_ff_kernel(a_ref, b_ref, c_ref, d_ref, gain_ref, w_ref, out_ref):
    x = a_ref[...].astype(F32) + b_ref[...].astype(F32)
    x = x + c_ref[...].astype(F32) + d_ref[...].astype(F32)
    mean = jnp.sum(x * x, axis=1, keepdims=True) / DD
    xn = (x * lax.rsqrt(mean + eps) * gain_ref[...]).astype(BF)
    acc = x * (1.0 / Y)
    wide = 2 * HID_PAD
    for i in range(4):
        w = w_ref.at[2 * i : 2 * i + 2]
        gate = dot_nt(xn, w[:, :wide].reshape(2 * wide, DD))
        upper = dot_nt(xn, w[:, wide : 2 * wide].reshape(2 * wide, DD))
        act = (jax.nn.silu(gate) * upper).astype(BF)
        acc += jnp.dot(
            act, w[:, 2 * wide :].reshape(2 * wide, DD), preferred_element_type=F32
        )
    for block in range(Z):
        turned = acc[:, block * 128 : (block + 1) * 128].T
        out_ref[block] = turned.reshape(Y, 32, 128).astype(BF)


def per_device(
    hidden_in,
    norm_gain,
    w_qkv,
    w_out,
    cache_keys,
    cache_values,
    lengths,
    tokens,
    w_in,
    embed,
    depth_gain,
    w_gate_up,
    w_down,
):
    xi, zi, yi, ci = (lax.axis_index(a) for a in ("cb", "z", "y", "core"))
    other = 1 - ci

    with jax.named_scope("gather_hidden"):
        hid_split, emb_sent = prepare(hidden_in.T, embed.transpose(0, 2, 1), tokens.T)
        gain_row = jnp.pad(norm_gain[None, :], ((0, 7), (0, 64)))
        copies = jnp.concatenate(
            [
                jnp.broadcast_to(hid_split[None], (Z, C, 64, 128)),
                jnp.broadcast_to(gain_row, (Z, C, 8, 128)),
                emb_sent,
            ],
            axis=2,
        )
        column = exchange(copies.reshape(16, 88, 128), ("z", "core")).reshape(Z, C, 88, 128)
        emb_here = column[:, :, 72:]
        started = swap(hid_split[0, :16])
        w_in, w_out, w_gate_up, w_down, w_qkv, started = lax.optimization_barrier(
            (w_in, w_out, w_gate_up, w_down, w_qkv, started)
        )

    with jax.named_scope("pack_weights"):
        recv_a = swap(pick(w_in, other))
        wo = lax.dynamic_slice_in_dim(w_out, xi * DD, DD, 1)
        first_in = jnp.concatenate([pick(w_in, ci), recv_a, wo], axis=0)
        gu_t = w_gate_up.transpose(0, 3, 1, 2)
        gap = ((0, HID_PAD - HID), (0, 0))

        def stacked(step):
            gu = pick(gu_t, step)
            parts = (gu[:, 0], gu[:, 1], pick(w_down, step))
            return [jnp.pad(part, gap) for part in parts]

        recv_b = swap(jnp.concatenate(stacked(other), axis=0))
        second_in = []
        for index, part in enumerate(stacked(ci)):
            second_in += [part, recv_b[index * HID_PAD : (index + 1) * HID_PAD]]
        second_in = jnp.concatenate(second_in, axis=0)
        first = lax.all_gather(first_in, "z")
        second = lax.all_gather(second_in, "z")

    with jax.named_scope("norm"):
        w_own = w_qkv.transpose(0, 2, 1).reshape(192, D)
        w_oth = swap(w_own)
        gains = jnp.pad(column[:, :, 64, :64].reshape(Z, 128), ((0, 8), (0, 0)))
        low = jnp.concatenate([column[:4, :, :64].reshape(512, 128), gains], axis=0)
        high = column[4:, :, :64].reshape(512, 128)
        others = ring_halves(low, high, "y")

    with jax.named_scope("qkv"):
        hid_cols = pick(column, zi)[:, :64].reshape(128, 128)
        sent = in_vmem(
            qkv_kernel,
            (128, 512),
            2 * 128 * 384 * D,
            (low, high, *others[0], *others[1], *others[2], w_own, w_oth, hid_cols),
        )
        got = exchange(sent.reshape(32, 4, 512), ("z", "y"))
        got = got.reshape(HEADS, 4, 4, HEAD_DIM).transpose(1, 2, 0, 3)

    with jax.named_scope("embed"):
        moved_emb = lax.ppermute(
            emb_here, ("cb", "core"), [(2 * x, 2 * ((x + 1) % X)) for x in range(X)]
        )
        emb = jnp.where(ci == 0, moved_emb, emb_here).reshape(256, 128)
        source = lax.broadcasted_iota(jnp.int32, (256, DD), 0)
        target = lax.broadcasted_iota(jnp.int32, (256, DD), 1)
        place = (target == (source // 32) * 128 + yi * 32 + source % 32).astype(BF)
        emb = jnp.dot(emb.T, place, preferred_element_type=F32).astype(BF)

    with jax.named_scope("attend"):
        got, first, wo_all = lax.optimization_barrier((got, first, first[:, 128:]))
        query_h, key_new, value_new = got[:, 0], got[:, 1], got[:, 2]
        hid_rows = got[:, 3]
        scale = 1.0 / math.sqrt(HEAD_DIM)
        keys_h = cache_keys.reshape(4, CACHE, HEADS, HEAD_DIM)
        values_h = cache_values.reshape(4, CACHE, HEADS, HEAD_DIM)
        scores = jnp.einsum("rhe,rphe->rhp", query_h, keys_h, preferred_element_type=F32) * scale
        live = lax.broadcasted_iota(jnp.int32, (1, 1, CACHE), 2) < lengths[:, None, None]
        scores = jnp.where(live, scores, -1e30)
        fresh = jnp.sum(query_h.astype(F32) * key_new.astype(F32), axis=-1) * scale
        top = jnp.maximum(jnp.max(scores, axis=-1), fresh)
        weights = jnp.exp(scores - top[..., None])
        weight_new = jnp.exp(fresh - top)
        total = jnp.sum(weights, axis=-1) + weight_new
        probs = (weights / total[..., None]).astype(BF)
        prob_new = (weight_new / total).astype(BF)
        mixed = jnp.einsum("rhp,rphe->rhe", probs, values_h, preferred_element_type=F32)
        mixed = mixed + prob_new.astype(F32)[..., None] * value_new.astype(F32)
        attended = mixed.astype(BF)

    with jax.named_scope("project"):
        att = attended.reshape(4, Z, Y, C, 64).transpose(2, 3, 0, 1, 4).reshape(1, 8, 4, 512)
        att = jnp.broadcast_to(att, (X, 8, 4, 512))
        res = hid_rows.reshape(4, X, 2, Y, C, 64).transpose(1, 3, 4, 0, 2, 5)
        res = res.reshape(X, 8, 4, 128)
        moved = exchange(
            jnp.concatenate([att, res], axis=-1).reshape(32, 4, 640), ("cb", "y", "core")
        ).reshape(128, 640)
        part = in_vmem(project_kernel, (8, 128, 128), 2 * 128 * 512 * DD, (moved[:, :512], wo_all))
        part = exchange(part, ("y", "core"))
        temporal = jnp.sum(part.astype(F32), axis=0) + moved[:, 512:].astype(F32)
        temporal = temporal.astype(BF)
        around = from_each(temporal, "cb")
        frame = jnp.zeros((X, 128, 128), BF)
        for step, piece in enumerate(around):
            at = lax.rem(xi - step + X, X)
            frame = lax.dynamic_update_slice(frame, piece[None], (at, 0, 0))
        frame_oth = swap(frame)

    with jax.named_scope("depth"):
        x_part = in_vmem(
            depth_in_kernel, (128, DD), 2 * 128 * 1024 * DD, (frame, frame_oth, first, emb)
        )
        rows = lax.dynamic_slice_in_dim(frame, xi * 32, 32, 1)
        rows = rows.reshape(X, 2, 16, 2, 64).transpose(0, 3, 2, 1, 4).reshape(Z, 16, 128)
        rows, second = lax.optimization_barrier((rows, second))
        gain_d = lax.dynamic_slice_in_dim(depth_gain, ci, 1, 0).astype(F32)
        out = in_vmem(
            depth_ff_kernel,
            (Z, Y, 32, 128),
            6 * 128 * 768 * DD,
            (*from_each(x_part, "y"), gain_d, second),
        )
        out = exchange(out.reshape(64, 16, 128), TP).reshape(Z, Y, C, 16, 128)
        out = jnp.sum(out.astype(F32), axis=1).astype(BF)

    with jax.named_scope("place_outputs"):
        depth_out = out.reshape(Z, C, 16, X, 32).transpose(1, 3, 0, 4, 2)
        depth_out = depth_out.reshape(C, 1024, 16)
        rows = exchange(rows, "z")
        temporal_out = rows.reshape(Z, 16, 2, 64).transpose(0, 2, 1, 3).reshape(256, 64)
    return (temporal_out, depth_out)


def solution(mesh):
    fine = Mesh(mesh.devices.reshape(X, Z, Y, C), ("cb", "z", "y", "core"))
    every = ("cb",) + TP
    in_specs = (
        P("cb", TP),
        P(TP),
        P(None, None, TP),
        P(TP, None),
        P(every, None, None),
        P(every, None, None),
        P(every),
        P(None, "cb"),
        P("cb", TP, None),
        P("cb", None, TP),
        P("cb", None),
        P("cb", None, None, TP),
        P("cb", TP, None),
    )
    out_specs = (P("cb", TP), P("cb", None, TP))
    return jax.shard_map(
        per_device, mesh=fine, in_specs=in_specs, out_specs=out_specs, check_vma=False
    )
```
